128 devices in a mesh: row: 4 (over x), col: 2 (over core), depth: 16 (over z, y).
Axes of the slice: x: 4, y: 4, z: 4, core: 2. Of those that a mesh axis runs over, the one named last changes fastest.
Arguments:
- inputs: bfloat16 [2048, 6144], P('depth', 'row'), may hold values from -6 to 6
- weight: bfloat16 [6144, 24576], P('row', 'col'), may hold values from -0.078125 to 0.078125
- bias: float32 [24576], P('col'), may hold values from -3 to 3
- cotangent: bfloat16 [2048, 24576], P(('depth', 'row'), 'col'), may hold values from -16 to 16
Outputs:
- activated: bfloat16 [2048, 24576], P(('depth', 'row'), 'col')
- input_grad: bfloat16 [2048, 6144], P('depth', ('row', 'col'))
- weight_grad: float32 [6144, 24576], P('row', ('col', 'depth'))
The draws below stay inside these ranges and needn't reach their ends.
All inputs are finite; a program needn't handle non-finite values.
Results may differ from the reference program's by a relative error of at most 0.0049.
Values may be sent and summed in bfloat16 or wider, within the bound.
No kernel may reach another device: no remote copies, remote signals or barrier semaphores. Data moves between devices by JAX's collectives and lax.ppermute only.
A program may use at most 256 MiB of HBM per device.

```python
import math
import jax
import jax.numpy as jnp
from jax import lax

D = 6144
F = 24576
TOKENS = 2048


def spiked(entries, rng, source, target, blocks, factor):
    def block_of(dim):
        return (jnp.arange(entries.shape[dim]) // (entries.shape[dim] // blocks)).reshape((-1,) + (1,) * (entries.ndim - 1 - dim))

    first = jax.random.permutation(rng, blocks)[block_of(target)]
    second = (block_of(target) + blocks // 2) % blocks
    return jnp.where((block_of(source) == first) | (block_of(source) == second), factor * entries, entries)


def block_levels(stream_key, shape, split, least, top_value):
    def one(axis_at, blocks):
        draws = jax.random.uniform(jax.random.fold_in(jax.random.fold_in(stream_key, 6), axis_at), (blocks,), jnp.float32, least / len(split), top_value / len(split))
        return jnp.repeat(jnp.exp(draws), shape[axis_at] // blocks).reshape((-1,) + (1,) * (len(shape) - axis_at - 1))

    gain = one(*split[0])
    for cut in split[1:]:
        gain = gain * one(*cut)
    return gain


def noise(rng, shape, deviation, most, cuts=(), dtype=jnp.bfloat16):
    array = jax.random.normal(rng, shape, jnp.float32) * deviation
    if len(cuts) > 0:
        array = block_levels(rng, shape, cuts, -0.22, 0.18) * array
    return jnp.clip(array, min=-most, max=most).astype(dtype)


def bell_draw_with(rng, dims, scale, bound, pieces, heavy, held_as=jnp.bfloat16):
    values = scale * jax.random.normal(rng, dims, jnp.float32)
    if pieces:
        values = values * block_levels(rng, dims, pieces, -0.22, 0.18)
    return jnp.clip(spiked(values, jax.random.fold_in(rng, 3), *heavy), -bound, bound).astype(held_as)


def setup_inputs(seed: int = 0) -> dict:
    splits = jax.random.split(jax.random.key(seed), 5)
    inputs = noise(splits[0], (TOKENS, D), 1.0, 6.0, ((0, 16), (1, 4)))
    weight = noise(splits[1], (D, F), D ** -0.5, 0.078125, ((0, 4), (1, 2)))
    bias = noise(splits[2], (F,), 0.5, 3.0, ((0, 2),), jnp.float32)
    cotangent = bell_draw_with(splits[3], (TOKENS, F), 1.0, 16.0, ((0, 64), (1, 2)), (0, 1, 64, 4.0))
    return {"inputs": inputs, "weight": weight, "bias": bias, "cotangent": cotangent}


def gelu_parts(pre):
    cdf = 0.5 * (1.0 + lax.erf(pre / math.sqrt(2.0)))
    dens = jnp.exp(-0.5 * pre * pre) / math.sqrt(2.0 * math.pi)
    return (pre * cdf, cdf + pre * dens)

def reference(inputs, weight, bias, cotangent):
    pre = jnp.dot(inputs, weight, preferred_element_type=jnp.float32) + bias.astype(jnp.float32)
    value, slope = gelu_parts(pre)
    activated = value.astype(jnp.bfloat16)
    pre_grad = (cotangent.astype(jnp.float32) * slope).astype(jnp.bfloat16)
    input_grad = lax.dot_general(pre_grad, weight, (((1,), (1,)), ((), ())), preferred_element_type=jnp.float32).astype(jnp.bfloat16)
    weight_grad = lax.dot_general(inputs, pre_grad, (((0,), (0,)), ((), ())), preferred_element_type=jnp.float32)
    weight_grad = weight_grad * float(TOKENS) ** (-0.5)
    return (activated, input_grad, weight_grad)
```

```python
import functools
import math

import jax
import jax.numpy as jnp
from jax import lax
from jax.experimental import pallas as pl
from jax.experimental.pallas import tpu as pltpu
from jax.sharding import PartitionSpec as P

BF = jnp.bfloat16
F32 = jnp.float32
ROWS, COLS, SIDE = 4, 2, 4
CHUNKS = ((1, 2), (3, 0))

RING = [
    (r * 2 + c, ((r + 1 - 2 * c) % ROWS) * 2 + c) for r in range(ROWS) for c in range(COLS)
]


def ring(v):
    return lax.ppermute(v, ("row", "col"), RING)


def shift_z(v, k):
    pairs = [(z * 4 + y, ((z + k) % 4) * 4 + y) for z in range(4) for y in range(4)]
    return lax.ppermute(v, "depth", pairs)


def shift_y(v, k):
    pairs = [(z * 4 + y, z * 4 + (y + k) % 4) for z in range(4) for y in range(4)]
    return lax.ppermute(v, "depth", pairs)


def swap(v):
    return lax.ppermute(v, "col", [(0, 1), (1, 0)])


def params(mib):
    return pltpu.CompilerParams(vmem_limit_bytes=mib << 20)


def cost(flops, moved, trans=0):
    return pl.CostEstimate(flops=flops, bytes_accessed=moved, transcendentals=trans)


def forward_body(blocks, x, w, own, first, second, third):
    part = jnp.dot(x[...], w[...], preferred_element_type=F32)
    n = own.shape[1]
    own[0] = part[:n]
    first[0] = part[n : 2 * n].astype(BF)
    second[0] = part[2 * n : 3 * n]
    third[0] = part[3 * n :]


def forward(blocks, x, w, width):
    count, (tokens, feats) = blocks.shape[0], x.shape
    n = tokens // ROWS
    out = pl.BlockSpec((1, n, width), lambda i, b: (i, 0, 0))
    shape = (count, n, width)
    return pl.pallas_call(
        forward_body,
        grid_spec=pltpu.PrefetchScalarGridSpec(
            num_scalar_prefetch=1,
            grid=(count,),
            in_specs=[
                pl.BlockSpec((tokens, feats), lambda i, b: (0, 0)),
                pl.BlockSpec((feats, width), lambda i, b: (0, b[i])),
            ],
            out_specs=[out] * 4,
        ),
        out_shape=[jax.ShapeDtypeStruct(shape, d) for d in (F32, BF, F32, F32)],
        compiler_params=params(24),
        cost_estimate=cost(2 * tokens * feats * width * count, 2 * feats * width * count),
        name="forward",
    )(blocks, x, w)


def gelu_body(blocks, got, own, bias, cot, *rest):
    grad, act = rest[-2:]
    pre = got[0].astype(F32) + own[0] + bias[...]
    cdf = 0.5 * (1.0 + lax.erf(pre / math.sqrt(2.0)))
    dens = jnp.exp(-0.5 * pre * pre) / math.sqrt(2.0 * math.pi)
    act[...] = (pre * cdf).astype(BF)
    grad[0] = (cot[...].astype(F32) * (cdf + pre * dens)).astype(BF)


def gelu(blocks, got, own, bias, cot, act):
    count, n, width = own.shape
    block = pl.BlockSpec((1, n, width), lambda i, b: (i, 0, 0))
    wide = pl.BlockSpec((n, width), lambda i, b: (0, b[i]))
    extra = [] if act is None else [act]
    return pl.pallas_call(
        gelu_body,
        grid_spec=pltpu.PrefetchScalarGridSpec(
            num_scalar_prefetch=1,
            grid=(count,),
            in_specs=[
                block,
                block,
                pl.BlockSpec((1, width), lambda i, b: (0, b[i])),
                wide,
            ]
            + [pl.BlockSpec(memory_space=pl.ANY)] * len(extra),
            out_specs=[block, wide],
        ),
        out_shape=[
            jax.ShapeDtypeStruct((count, n, width), BF),
            jax.ShapeDtypeStruct(cot.shape, BF),
        ],
        input_output_aliases={5: 1} if extra else {},
        compiler_params=params(16),
        cost_estimate=cost(60 * count * n * width, 10 * count * n * width, count * n * width),
        name="gelu",
    )(blocks, got, own, bias, cot, *extra)


def input_body(last, scalars, g0, g1, g2, g3, w, *rest):
    i = pl.program_id(0)
    grad = jnp.concatenate([g0[0], g1[0], g2[0], g3[0]], axis=0)
    n, half = g0.shape[1], w.shape[0] // 2
    outs = rest[1:] if last else rest
    total = outs[-1]

    @pl.when(i == 0)
    def _():
        if last:
            total[...] = rest[0][...]
        else:
            total[...] = jnp.zeros_like(total)

    for h in range(2):
        total[h] += lax.dot_general(
            grad,
            w[h * half : (h + 1) * half, :],
            (((1,), (1,)), ((), ())),
            preferred_element_type=F32,
        )

    @pl.when(i == pl.num_programs(0) - 1)
    def _():
        if last:
            col = scalars[pl.num_programs(0) + ROWS]
            for k in range(ROWS):
                place = pl.multiple_of(scalars[pl.num_programs(0) + k] * n, n)
                outs[0][pl.ds(place, n), :] = total[col, k * n : (k + 1) * n, :]
                outs[1][pl.ds(place, n), :] = total[1 - col, k * n : (k + 1) * n, :]
        else:
            outs[0][...] = total[...]


def input_grads(scalars, grads, w, before):
    count, n, width = grads[0].shape
    feats, last = w.shape[0], before is not None
    tokens = ROWS * n
    block = pl.BlockSpec((1, n, width), lambda i, b: (i, 0, 0))
    acc = (2, tokens, feats // 2)
    whole = pl.BlockSpec(acc, lambda i, b: (0, 0, 0))
    one = pl.BlockSpec(acc[1:], lambda i, b: (0, 0))
    return pl.pallas_call(
        functools.partial(input_body, last),
        grid_spec=pltpu.PrefetchScalarGridSpec(
            num_scalar_prefetch=1,
            grid=(count,),
            in_specs=[block] * 4
            + [pl.BlockSpec((feats, width), lambda i, b: (0, b[i]))]
            + ([whole] if last else []),
            out_specs=[one, one] if last else [whole],
            scratch_shapes=[pltpu.VMEM(acc, F32)],
        ),
        out_shape=[jax.ShapeDtypeStruct(acc[1:], F32)] * 2
        if last
        else [jax.ShapeDtypeStruct(acc, F32)],
        compiler_params=params(24),
        cost_estimate=cost(2 * tokens * feats * width * count, 2 * feats * width * count),
        name="input_grads",
    )(scalars, *grads, w, *([before] if last else []))


def weight_body(factor, scalars, mine, other, g0, g1, g2, g3, out):
    def run(x, way):
        total = None
        for k, g in enumerate((g0, g1, g2, g3)):
            lhs = x[:, way * k % ROWS].reshape(-1, x.shape[-1])
            rhs = g[...].reshape(-1, g.shape[-1])
            part = lax.dot_general(
                lhs, rhs, (((0,), (0,)), ((), ())), preferred_element_type=F32
            )
            total = part if total is None else total + part
        out[...] = total * factor

    first = pl.program_id(0) < pl.num_programs(0) // 2

    @pl.when(first)
    def _():
        run(mine, 1)

    @pl.when(jnp.logical_not(first))
    def _():
        run(other, -1)


def weight_grads(col, mine, other, grads, tile, factor):
    groups, _, n, half = mine.shape
    width = grads[0].shape[-1]
    steps = half // tile
    g = pl.BlockSpec((groups, n, width), lambda i, b: (0, 0, 0))
    return pl.pallas_call(
        functools.partial(weight_body, factor),
        grid_spec=pltpu.PrefetchScalarGridSpec(
            num_scalar_prefetch=1,
            grid=(2 * steps,),
            in_specs=[
                pl.BlockSpec(
                    (groups, ROWS, n, tile), lambda i, b: (0, 0, 0, jnp.minimum(i, steps - 1))
                ),
                pl.BlockSpec(
                    (groups, ROWS, n, tile), lambda i, b: (0, 0, 0, jnp.maximum(i - steps, 0))
                ),
                g,
                g,
                g,
                g,
            ],
            out_specs=pl.BlockSpec(
                (tile, width),
                lambda i, b: (
                    jnp.where(i < steps, b[0] * steps + i, (1 - b[0]) * steps + i - steps),
                    0,
                ),
            ),
        ),
        out_shape=jax.ShapeDtypeStruct((2 * half, width), F32),
        compiler_params=params(32),
        cost_estimate=cost(
            4 * groups * ROWS * n * half * width, 4 * groups * ROWS * n * (half + width)
        ),
        name="weight_grads",
    )(col, mine, other, *grads)


def shards(inputs, weight, bias, cotangent):
    tok, feats = inputs.shape
    n = tok // ROWS
    groups = SIDE * SIDE
    width = weight.shape[1] // groups
    r, c, d = lax.axis_index("row"), lax.axis_index("col"), lax.axis_index("depth")
    z, y = d // SIDE, d % SIDE
    way = 1 - 2 * c
    order = [(r - way * k + 2 * ROWS) % ROWS for k in range(ROWS)]
    x = jnp.concatenate(
        [lax.dynamic_slice_in_dim(inputs, b * n, n, 0) for b in order], axis=0
    )
    bias = bias.reshape(1, -1)
    chunks = [
        jnp.stack(
            [((z + kz) % SIDE) * SIDE + (y + ky) % SIDE for kz in chunk for ky in range(SIDE)]
        ).astype(jnp.int32)
        for chunk in CHUNKS
    ]
    tail = jnp.stack(order + [c]).astype(jnp.int32)

    parts = [forward(blocks, x, weight, width) for blocks in chunks]
    act, grads = None, []
    for blocks, (own, first, second, third) in zip(chunks, parts):
        got = ring(first)
        got = ring((got.astype(F32) + second).astype(BF))
        got = ring((got.astype(F32) + third).astype(BF))
        grad, act = gelu(blocks, got, own, bias, cotangent, act)
        grads.append(grad)

    half = lax.dynamic_slice_in_dim(x, c * (feats // 2), feats // 2, 1).reshape(
        1, ROWS, n, feats // 2
    )
    column = jnp.stack([half] + [shift_z(half, k) for k in range(1, SIDE)], axis=1)
    mine = jnp.concatenate([column] + [shift_y(column, k) for k in range(1, SIDE)], axis=0)
    mine = mine.reshape(groups, ROWS, n, feats // 2)
    other = swap(mine)

    at = {}
    for chunk, grad in zip(CHUNKS, grads):
        for j, kz in enumerate(chunk):
            piece = grad[j * SIDE : (j + 1) * SIDE]
            at[kz] = piece if kz == 0 else shift_z(piece, kz)
    held = [jnp.stack([at[kz][ky] for kz in range(SIDE)]) for ky in range(SIDE)]
    held = [held[0]] + [shift_y(held[k], k) for k in range(1, SIDE)]
    rows = [jnp.stack(held).reshape(groups, n, width)]

    before = None
    for blocks, grad in zip(chunks, grads):
        line = [grad]
        for _ in range(ROWS - 1):
            line.append(ring(line[-1]))
        out = input_grads(jnp.concatenate([blocks, tail]), line, weight, before)
        before = out[0]
    own_part, other_part = out
    input_grad = (own_part + swap(other_part)).astype(BF)

    for _ in range(ROWS - 1):
        rows.append(ring(rows[-1]))
    factor = float(tok * lax.axis_size("depth")) ** (-0.5)
    weight_grad = weight_grads(tail[ROWS:], mine, other, rows, 256, factor)
    return (act, input_grad, weight_grad)


def solution(mesh):
    return jax.shard_map(
        shards,
        mesh=mesh,
        in_specs=(P("depth", "row"), P("row", "col"), P("col"), P(("depth", "row"), "col")),
        out_specs=(
            P(("depth", "row"), "col"),
            P("depth", ("row", "col")),
            P("row", ("col", "depth")),
        ),
        check_vma=False,
    )
```

```python
import functools
import math

import jax
import jax.numpy as jnp
from jax import lax
from jax.experimental import pallas as pl
from jax.experimental.pallas import tpu as pltpu
from jax.sharding import PartitionSpec as P

BF = jnp.bfloat16
F32 = jnp.float32
ROWS, COLS, SIDE = 4, 2, 4
CHUNKS = ((1, 3), (2, 0))
FREE = pl.CostEstimate(flops=0, bytes_accessed=0, transcendentals=0)


RING = [
    (r * 2 + c, (r + 1 - 2 * c) % ROWS * 2 + c) for r in range(ROWS) for c in range(COLS)
]


def shift(k, along_z):
    pairs = []
    for c in range(COLS):
        way = k * (1 - 2 * c)
        for z in range(SIDE):
            for y in range(SIDE):
                to = (z + way) % SIDE * 4 + y if along_z else z * 4 + (y + way) % SIDE
                pairs.append((c * 16 + z * 4 + y, c * 16 + to))
    return pairs


def ring(v):
    return lax.ppermute(v, ("row", "col"), RING)


def shift_z(v, k):
    return lax.ppermute(v, ("col", "depth"), shift(k, True))


def shift_y(v, k):
    return lax.ppermute(v, ("col", "depth"), shift(k, False))


def swap(v):
    return lax.ppermute(v, "col", [(0, 1), (1, 0)])


def untouched(*refs):
    pass


def after(v, *earlier):
    anywhere = pl.BlockSpec(memory_space=pl.ANY)
    return pl.pallas_call(
        untouched,
        in_specs=[anywhere] * (1 + len(earlier)),
        out_specs=anywhere,
        out_shape=jax.ShapeDtypeStruct(v.shape, v.dtype),
        input_output_aliases={0: 0},
        compiler_params=params(1),
        cost_estimate=FREE,
        name="after",
    )(v, *earlier)


def waiting(body, count, inputs):
    def inner(*refs):
        return body(*refs[:inputs], *refs[inputs + count :])

    return inner


def params(mib):
    return pltpu.CompilerParams(vmem_limit_bytes=mib << 20)


def forward_body(with_half, s, x, w, own, first, second, third, token, *rest):
    n, width = own.shape[1:]
    steps = pl.num_programs(0)
    rows = rest[-1]

    @pl.when(pl.program_id(0) == 0)
    def _():
        for k in range(ROWS):
            rows[k * n : (k + 1) * n, :] = x[
                pl.ds(pl.multiple_of(s[steps + k] * n, n), n), :
            ]
        if with_half:
            half = x.shape[1] // 2
            at = pl.multiple_of(s[steps + ROWS] * half, half)
            for k in range(ROWS):
                rest[0][0, 0, k] = rows[k * n : (k + 1) * n, pl.ds(at, half)]
        token[...] = jnp.zeros_like(token)

    part = jnp.dot(rows[...], w[...], preferred_element_type=F32)
    for j in range(own.shape[0]):
        cut = part[:, j * width : (j + 1) * width]
        own[j] = cut[:n]
        first[j] = cut[n : 2 * n].astype(BF)
        second[j] = cut[2 * n : 3 * n]
        third[j] = cut[3 * n :]


TOKEN = jax.ShapeDtypeStruct((8, 128), F32)


def token_spec():
    return pl.BlockSpec((8, 128), lambda i, s: (0, 0))


def forward(scalars, x, w, width, with_half, *earlier):
    count, (tokens, feats) = scalars.shape[0] - ROWS - 1, x.shape
    n = tokens // ROWS
    out = pl.BlockSpec((2, n, width), lambda i, s: (i, 0, 0))
    shape = (2 * count, n, width)
    half = (1, 1, ROWS, n, feats // 2)
    return pl.pallas_call(
        waiting(functools.partial(forward_body, with_half), len(earlier), 3),
        grid_spec=pltpu.PrefetchScalarGridSpec(
            num_scalar_prefetch=1,
            grid=(count,),
            in_specs=[
                pl.BlockSpec((tokens, feats), lambda i, s: (0, 0)),
                pl.BlockSpec((feats, 2 * width), lambda i, s: (0, s[i])),
            ]
            + [pl.BlockSpec(memory_space=pl.ANY)] * len(earlier),
            out_specs=[out] * 4
            + [token_spec()]
            + [pl.BlockSpec(half, lambda i, s: (0, 0, 0, 0, 0))] * with_half,
            scratch_shapes=[pltpu.VMEM((tokens, feats), BF)],
        ),
        out_shape=[jax.ShapeDtypeStruct(shape, d) for d in (F32, BF, F32, F32)]
        + [TOKEN]
        + [jax.ShapeDtypeStruct(half, BF)] * with_half,
        compiler_params=params(20),
        cost_estimate=FREE,
        name="forward",
    )(scalars, x, w, *earlier)


def gelu_body(s, got, own, bias, cot, *rest):
    grad, act = rest[-2:]
    width = own.shape[2]
    for j in range(own.shape[0]):
        at = slice(j * width, (j + 1) * width)
        pre = got[j].astype(F32) + own[j] + bias[:, at]
        cdf = 0.5 * (1.0 + lax.erf(pre / math.sqrt(2.0)))
        dens = jnp.exp(-0.5 * pre * pre) / math.sqrt(2.0 * math.pi)
        act[:, at] = (pre * cdf).astype(BF)
        grad[j] = (cot[:, at].astype(F32) * (cdf + pre * dens)).astype(BF)


def gelu(scalars, got, own, bias, cot, act, *earlier):
    count, n, width = own.shape
    block = pl.BlockSpec((SIDE, n, width), lambda i, s: (i, 0, 0))
    wide = pl.BlockSpec((n, SIDE * width), lambda i, s: (0, s[2 * i] // 2))
    extra = [*([] if act is None else [act]), *earlier]
    return pl.pallas_call(
        gelu_body,
        grid_spec=pltpu.PrefetchScalarGridSpec(
            num_scalar_prefetch=1,
            grid=(count // SIDE,),
            in_specs=[
                block,
                block,
                pl.BlockSpec((1, SIDE * width), lambda i, s: (0, s[2 * i] // 2)),
                wide,
            ]
            + [pl.BlockSpec(memory_space=pl.ANY)] * len(extra),
            out_specs=[block, wide],
        ),
        out_shape=[
            jax.ShapeDtypeStruct((count, n, width), BF),
            jax.ShapeDtypeStruct(cot.shape, BF),
        ],
        input_output_aliases={} if act is None else {5: 1},
        compiler_params=params(8),
        cost_estimate=FREE,
        name="gelu",
    )(scalars, got, own, bias, cot, *extra)


def input_body(last, s, g0, g1, g2, g3, w, *rest):
    i, steps = pl.program_id(0), pl.num_programs(0)
    n = g0.shape[1]
    grad = jnp.concatenate(
        [jnp.concatenate([g[j] for j in range(g.shape[0])], axis=1) for g in (g0, g1, g2, g3)],
        axis=0,
    )
    total, token = rest[-1], rest[-2]
    part = lax.dot_general(
        w[...], grad, (((1,), (1,)), ((), ())), preferred_element_type=F32
    )

    @pl.when(i == 0)
    def _():
        total[...] = part + rest[0][...] if last else part
        token[...] = jnp.zeros_like(token)

    @pl.when(i > 0)
    def _():
        total[...] += part

    @pl.when(i == steps - 1)
    def _():
        if last:
            half = total.shape[0] // 2
            col = s[steps + ROWS]
            for out, h in ((rest[1], col), (rest[2], 1 - col)):
                rows = total[pl.ds(pl.multiple_of(h * half, half), half), :].T
                for k in range(ROWS):
                    place = pl.multiple_of(s[steps + k] * n, n)
                    out[pl.ds(place, n), :] = rows[k * n : (k + 1) * n, :]
        else:
            rest[0][...] = total[...]


def input_grads(scalars, grads, w, before, *earlier):
    count, n, width = grads[0].shape
    feats, last = w.shape[0], before is not None
    tokens = ROWS * n
    block = pl.BlockSpec((2, n, width), lambda i, s: (i, 0, 0))
    acc = (feats, tokens)
    whole = pl.BlockSpec(acc, lambda i, s: (0, 0))
    shape = (tokens, feats // 2)
    one = pl.BlockSpec(shape, lambda i, s: (0, 0))
    return pl.pallas_call(
        waiting(functools.partial(input_body, last), len(earlier), 7 if last else 6),
        grid_spec=pltpu.PrefetchScalarGridSpec(
            num_scalar_prefetch=1,
            grid=(count // 2,),
            in_specs=[block] * 4
            + [pl.BlockSpec((feats, 2 * width), lambda i, s: (0, s[i]))]
            + ([whole] if last else [])
            + [pl.BlockSpec(memory_space=pl.ANY)] * len(earlier),
            out_specs=([one, one] if last else [whole]) + [token_spec()],
            scratch_shapes=[pltpu.VMEM(acc, F32)],
        ),
        out_shape=(
            [jax.ShapeDtypeStruct(shape, F32)] * 2
            if last
            else [jax.ShapeDtypeStruct(acc, F32)]
        )
        + [TOKEN],
        compiler_params=params(24),
        cost_estimate=FREE,
        name="input_grads",
    )(scalars, *grads, w, *([before] if last else []), *earlier)


def weight_body(factor, last, kzs, col, *refs):
    mine, other, grads = refs[:SIDE], refs[SIDE : 2 * SIDE], refs[2 * SIDE : 2 * SIDE + ROWS]
    rest = refs[2 * SIDE + ROWS :]
    out = rest[-1]

    def run(x, way):
        total = rest[0][...] if last else None
        for k, g in enumerate(grads):
            lhs = jnp.concatenate(
                [
                    x[way * ky % SIDE][0, kzs.index(way * kz % SIDE), way * k % ROWS]
                    for ky in range(SIDE)
                    for kz in kzs
                ],
                axis=0,
            )
            rhs = g[...].reshape(-1, g.shape[-1])
            part = lax.dot_general(
                lhs, rhs, (((0,), (0,)), ((), ())), preferred_element_type=F32
            )
            total = part if total is None else total + part
        out[...] = total * factor if last else total

    first = pl.program_id(0) < pl.num_programs(0) // 2

    @pl.when(first)
    def _():
        run(mine, 1)

    @pl.when(jnp.logical_not(first))
    def _():
        run(other, -1)


def weight_grads(col, j, mine, other, grads, before, tile, factor):
    side, depth, n, width = grads[0].shape
    half = mine[0].shape[-1]
    steps = half // tile
    last = before is not None
    g = pl.BlockSpec((side, depth, n, width), lambda i, s: (0, 0, 0, 0))
    x = (1, depth, ROWS, n, tile)
    out = pl.BlockSpec(
        (tile, width),
        lambda i, s: (
            jnp.where(i < steps, s[0] * steps + i, (1 - s[0]) * steps + i - steps),
            0,
        ),
    )
    return pl.pallas_call(
        functools.partial(weight_body, factor, last, CHUNKS[j]),
        grid_spec=pltpu.PrefetchScalarGridSpec(
            num_scalar_prefetch=1,
            grid=(2 * steps,),
            in_specs=[pl.BlockSpec(x, lambda i, s: (0, j, 0, 0, jnp.minimum(i, steps - 1)))]
            * SIDE
            + [pl.BlockSpec(x, lambda i, s: (0, j, 0, 0, jnp.maximum(i - steps, 0)))] * SIDE
            + [g] * ROWS
            + ([out] if last else []),
            out_specs=out,
        ),
        out_shape=jax.ShapeDtypeStruct((2 * half, width), F32),
        compiler_params=params(24),
        cost_estimate=FREE,
        name="weight_grads",
    )(col, *mine, *other, *grads, *([before] if last else []))


def shards(inputs, weight, bias, cotangent):
    tok, feats = inputs.shape
    n = tok // ROWS
    width = weight.shape[1] // (SIDE * SIDE)
    r, c, d = lax.axis_index("row"), lax.axis_index("col"), lax.axis_index("depth")
    z, y = d // SIDE, d % SIDE
    way = 1 - 2 * c
    order = [(r - way * k + 2 * ROWS) % ROWS for k in range(ROWS)]
    inputs = pltpu.with_memory_space_constraint(inputs, pltpu.HBM)
    bias = bias.reshape(1, -1)
    s0, s1 = [
        jnp.stack(
            [((z + way * kz + SIDE) % SIDE) * 2 + p for kz in chunk for p in range(2)] + order + [c]
        ).astype(jnp.int32)
        for chunk in CHUNKS
    ]
    col = jnp.stack([c]).astype(jnp.int32)
    ys = [(y + way * k + SIDE) % SIDE for k in range(SIDE)]

    def add(got, part):
        return (got.astype(F32) + part).astype(BF)

    def to_column(at, grad, chunk):
        return [
            (grad[j * SIDE : (j + 1) * SIDE] if kz == 0 else at[kz]) for j, kz in enumerate(chunk)
        ]

    def for_y(pieces, k):
        return jnp.stack(
            [lax.dynamic_index_in_dim(p, ys[k], 0, keepdims=False) for p in pieces]
        )

    own0, first0, second0, third0, token0, x = forward(s0, inputs, weight, width, True)
    r0 = ring(first0)
    x_z1 = shift_z(x, 1)
    own1, first1, second1, third1, token1 = forward(s1, inputs, weight, width, False, token0)
    sum0 = add(r0, after(second0, token1, x_z1))
    r0 = ring(sum0)
    r1 = ring(after(first1, sum0))
    x = jnp.concatenate([x, after(x_z1, token1)], axis=1)
    x_z2 = shift_z(x, 2)

    sum0 = add(r0, after(third0, x_z2))
    r0 = ring(sum0)
    sum1 = add(r1, second1)
    r1 = ring(sum1)
    x_z2 = after(x_z2, sum0)
    by_z = [x[:, 0], x[:, 1], x_z2[:, 0], x_z2[:, 1]]
    x = jnp.stack([by_z[kz] for chunk in CHUNKS for kz in chunk], axis=1)
    x_y2 = shift_y(x, 2)
    grad0, act = gelu(s0, r0, own0, bias, cotangent, None, sum1)
    line0 = [grad0, ring(grad0)]
    at0 = {kz: shift_z(grad0[j * SIDE : (j + 1) * SIDE], kz) for j, kz in enumerate(CHUNKS[0])}
    r1 = ring(add(r1, third1))
    grad1, act = gelu(s1, r1, own1, bias, cotangent, act)
    line0.append(ring(line0[1]))
    line1 = [grad1, ring(grad1)]
    at1 = {
        kz: shift_z(after(grad1[j * SIDE : (j + 1) * SIDE], *at0.values()), kz)
        for j, kz in enumerate(CHUNKS[1])
        if kz
    }
    x = after(x, x_y2, grad1)
    x_y1 = shift_y(x, 1)
    at1 = {kz: after(v, line0[2]) for kz, v in at1.items()}
    pieces = to_column(at0, grad0, CHUNKS[0]) + to_column(at1, grad1, CHUNKS[1])
    held = [for_y(pieces, k) for k in range(SIDE)]
    held = [held[0]] + [shift_y(held[k], k) for k in range(1, SIDE)]
    line0.append(ring(line0[2]))
    rows0 = [after(jnp.stack([h[:2] for h in held]), line1[1], line0[3])]
    rows1 = [after(jnp.stack([h[2:] for h in held]), line1[1])]
    x = after(x, x_y1, rows0[0])
    x_y3 = shift_y(x, 3)
    rows0.append(ring(rows0[0]))
    rows1.append(ring(rows1[0]))
    line1.append(ring(line1[1]))
    line1.append(ring(line1[2]))

    before, token = input_grads(s0, line0, weight, None, rows0[0])
    rows0.append(ring(after(rows0[1], token, line1[2])))
    rows1.append(ring(after(rows1[1], token)))
    mine = (x, x_y1, x_y2, x_y3)
    other = [swap(v) for v in mine]
    own_part, other_part, token = input_grads(s1, line1, weight, before)
    rows0.append(ring(after(rows0[2], token)))
    rows1.append(ring(after(rows1[2], token)))
    input_grad = (own_part + swap(other_part)).astype(BF)
    factor = float(tok * lax.axis_size("depth")) ** (-0.5)
    half_done = weight_grads(col, 0, mine, other, rows0, None, 256, factor)
    weight_grad = weight_grads(col, 1, mine, other, rows1, half_done, 256, factor)
    return (act, input_grad, weight_grad)


def solution(mesh):
    return jax.shard_map(
        shards,
        mesh=mesh,
        in_specs=(P("depth", "row"), P("row", "col"), P("col"), P(("depth", "row"), "col")),
        out_specs=(
            P(("depth", "row"), "col"),
            P("depth", ("row", "col")),
            P("row", ("col", "depth")),
        ),
        check_vma=False,
    )
```

```python
import functools
import math

import jax
import jax.numpy as jnp
from jax import lax
from jax.experimental import pallas as pl
from jax.experimental.pallas import tpu as pltpu
from jax.sharding import PartitionSpec as P

BF = jnp.bfloat16
F32 = jnp.float32
ROWS, COLS, SIDE = 4, 2, 4
CHUNKS = ((1, 3), (2, 0))
FREE = pl.CostEstimate(flops=0, bytes_accessed=0, transcendentals=0)


def shift(k, along):
    pairs = []
    for c in range(COLS):
        way = k * (1 - 2 * c)
        for at in range(ROWS if along == "row" else SIDE * SIDE):
            z, y = divmod(at, SIDE)
            if along == "row":
                pairs.append((at * COLS + c, (at + way) % ROWS * COLS + c))
            else:
                to = (z + way) % SIDE * SIDE + y if along == "z" else z * SIDE + (y + way) % SIDE
                pairs.append((c * SIDE * SIDE + at, c * SIDE * SIDE + to))
    return pairs


def shift_row(v, k):
    return lax.ppermute(v, ("row", "col"), shift(k, "row"))


def shift_z(v, k):
    return lax.ppermute(v, ("col", "depth"), shift(k, "z"))


def shift_y(v, k):
    return lax.ppermute(v, ("col", "depth"), shift(k, "y"))


def swap(v):
    return lax.ppermute(v, "col", [(0, 1), (1, 0)])


def untouched(*refs):
    pass


def after(v, *earlier):
    anywhere = pl.BlockSpec(memory_space=pl.ANY)
    return pl.pallas_call(
        untouched,
        in_specs=[anywhere] * (1 + len(earlier)),
        out_specs=anywhere,
        out_shape=jax.ShapeDtypeStruct(v.shape, v.dtype),
        input_output_aliases={0: 0},
        compiler_params=params(1),
        cost_estimate=FREE,
        name="after",
    )(v, *earlier)


def waiting(body, count, inputs):
    def inner(*refs):
        return body(*refs[:inputs], *refs[inputs + count :])

    return inner


def params(mib):
    return pltpu.CompilerParams(vmem_limit_bytes=mib << 20)


def forward_body(with_half, s, x, w, own, first, second, third, token, *rest):
    n, width = own.shape[1:]
    steps = pl.num_programs(0)
    rows = rest[-1]

    @pl.when(pl.program_id(0) == 0)
    def _():
        for k in range(ROWS):
            rows[k * n : (k + 1) * n, :] = x[
                pl.ds(pl.multiple_of(s[steps + k] * n, n), n), :
            ]
        if with_half:
            half = x.shape[1] // 2
            at = pl.multiple_of(s[steps + ROWS] * half, half)
            for k in range(ROWS):
                rest[0][0, k] = rows[k * n : (k + 1) * n, pl.ds(at, half)]
        token[...] = jnp.zeros_like(token)

    part = jnp.dot(rows[...], w[...], preferred_element_type=F32)
    for j in range(own.shape[0]):
        cut = part[:, j * width : (j + 1) * width]
        own[j] = cut[:n]
        for k, out in enumerate((first, second, third)):
            out[j] = cut[(k + 1) * n : (k + 2) * n].astype(BF)


TOKEN = jax.ShapeDtypeStruct((8, 128), F32)


def token_spec():
    return pl.BlockSpec((8, 128), lambda i, s: (0, 0))


def forward(scalars, x, w, width, with_half, *earlier):
    count, (tokens, feats) = scalars.shape[0] - ROWS - 1, x.shape
    n = tokens // ROWS
    out = pl.BlockSpec((2, n, width), lambda i, s: (i, 0, 0))
    shape = (2 * count, n, width)
    half = (1, ROWS, n, feats // 2)
    return pl.pallas_call(
        waiting(functools.partial(forward_body, with_half), len(earlier), 3),
        grid_spec=pltpu.PrefetchScalarGridSpec(
            num_scalar_prefetch=1,
            grid=(count,),
            in_specs=[
                pl.BlockSpec((tokens, feats), lambda i, s: (0, 0)),
                pl.BlockSpec((feats, 2 * width), lambda i, s: (0, s[i])),
            ]
            + [pl.BlockSpec(memory_space=pl.ANY)] * len(earlier),
            out_specs=[out] * 4
            + [token_spec()]
            + [pl.BlockSpec(half, lambda i, s: (0, 0, 0, 0))] * with_half,
            scratch_shapes=[pltpu.VMEM((tokens, feats), BF)],
        ),
        out_shape=[jax.ShapeDtypeStruct(shape, d) for d in (F32, BF, BF, BF)]
        + [TOKEN]
        + [jax.ShapeDtypeStruct(half, BF)] * with_half,
        compiler_params=params(20),
        cost_estimate=FREE,
        name="forward",
    )(scalars, x, w, *earlier)


def gelu_body(s, got1, got2, got3, own, bias, cot, *rest):
    grad, act = rest[-2:]
    width = own.shape[2]
    for j in range(own.shape[0]):
        at = slice(j * width, (j + 1) * width)
        pre = got1[j].astype(F32) + got2[j].astype(F32) + got3[j].astype(F32)
        pre = pre + own[j] + bias[:, at]
        cdf = 0.5 * (1.0 + lax.erf(pre / math.sqrt(2.0)))
        dens = jnp.exp(-0.5 * pre * pre) / math.sqrt(2.0 * math.pi)
        act[:, at] = (pre * cdf).astype(BF)
        grad[j] = (cot[:, at].astype(F32) * (cdf + pre * dens)).astype(BF)


def gelu(scalars, got, own, bias, cot, act, *earlier):
    count, n, width = own.shape
    block = pl.BlockSpec((SIDE, n, width), lambda i, s: (i, 0, 0))
    wide = pl.BlockSpec((n, SIDE * width), lambda i, s: (0, s[2 * i] // 2))
    extra = [*([] if act is None else [act]), *earlier]
    return pl.pallas_call(
        gelu_body,
        grid_spec=pltpu.PrefetchScalarGridSpec(
            num_scalar_prefetch=1,
            grid=(count // SIDE,),
            in_specs=[
                block,
                block,
                block,
                block,
                pl.BlockSpec((1, SIDE * width), lambda i, s: (0, s[2 * i] // 2)),
                wide,
            ]
            + [pl.BlockSpec(memory_space=pl.ANY)] * len(extra),
            out_specs=[block, wide],
        ),
        out_shape=[
            jax.ShapeDtypeStruct((count, n, width), BF),
            jax.ShapeDtypeStruct(cot.shape, BF),
        ],
        input_output_aliases={} if act is None else {7: 1},
        compiler_params=params(8),
        cost_estimate=FREE,
        name="gelu",
    )(scalars, *got, own, bias, cot, *extra)


def input_body(last, s, g0, g1, g2, g3, w, *rest):
    i, steps = pl.program_id(0), pl.num_programs(0)
    n = g0.shape[1]
    grad = jnp.concatenate(
        [jnp.concatenate([g[j] for j in range(g.shape[0])], axis=1) for g in (g0, g1, g2, g3)],
        axis=0,
    )
    total, token = rest[-1], rest[-2]
    part = lax.dot_general(
        w[...], grad, (((1,), (1,)), ((), ())), preferred_element_type=F32
    )

    @pl.when(i == 0)
    def _():
        total[...] = part + rest[0][...] if last else part
        token[...] = jnp.zeros_like(token)

    @pl.when(i > 0)
    def _():
        total[...] += part

    @pl.when(i == steps - 1)
    def _():
        if last:
            half = total.shape[0] // 2
            col = s[steps + ROWS]
            for out, h in ((rest[1], col), (rest[2], 1 - col)):
                rows = total[pl.ds(pl.multiple_of(h * half, half), half), :].T
                for k in range(ROWS):
                    place = pl.multiple_of(s[steps + k] * n, n)
                    out[pl.ds(place, n), :] = rows[k * n : (k + 1) * n, :]
        else:
            rest[0][...] = total[...]


def input_grads(scalars, grads, w, before, *earlier):
    count, n, width = grads[0].shape
    feats, last = w.shape[0], before is not None
    tokens = ROWS * n
    block = pl.BlockSpec((2, n, width), lambda i, s: (i, 0, 0))
    acc = (feats, tokens)
    whole = pl.BlockSpec(acc, lambda i, s: (0, 0))
    shape = (tokens, feats // 2)
    one = pl.BlockSpec(shape, lambda i, s: (0, 0))
    return pl.pallas_call(
        waiting(functools.partial(input_body, last), len(earlier), 7 if last else 6),
        grid_spec=pltpu.PrefetchScalarGridSpec(
            num_scalar_prefetch=1,
            grid=(count // 2,),
            in_specs=[block] * 4
            + [pl.BlockSpec((feats, 2 * width), lambda i, s: (0, s[i]))]
            + ([whole] if last else [])
            + [pl.BlockSpec(memory_space=pl.ANY)] * len(earlier),
            out_specs=([one, one] if last else [whole]) + [token_spec()],
            scratch_shapes=[pltpu.VMEM(acc, F32)],
        ),
        out_shape=(
            [jax.ShapeDtypeStruct(shape, F32)] * 2
            if last
            else [jax.ShapeDtypeStruct(acc, F32)]
        )
        + [TOKEN],
        compiler_params=params(24),
        cost_estimate=FREE,
        name="input_grads",
    )(scalars, *grads, w, *([before] if last else []), *earlier)


KZS = tuple(kz for chunk in CHUNKS for kz in chunk)


def weight_body(factor, ks, last, col, *refs):
    mine, other, refs = refs[:SIDE], refs[SIDE : 2 * SIDE], refs[2 * SIDE :]
    parts, before, out, rhs = refs[: -2 - last], refs[-2 - last], refs[-2], refs[-1]
    i, steps = pl.program_id(0), pl.num_programs(0) // 2
    n = parts[0].shape[2]
    rows = SIDE * SIDE * n

    @pl.when(i == 0)
    def _():
        at = 0
        for part in parts:
            for ky in range(part.shape[0]):
                for spot in range(SIDE):
                    rhs[at : at + n, :] = part[ky, spot]
                    at += n

    def run(x, way):
        total = None
        for j, k in enumerate(ks):
            lhs = jnp.concatenate(
                [
                    x[way * kz % SIDE][way * ky % SIDE, 0 if last else way * k % ROWS]
                    for ky in range(SIDE)
                    for kz in KZS
                ],
                axis=0,
            )
            part = lax.dot_general(
                lhs,
                rhs[j * rows : (j + 1) * rows, :],
                (((0,), (0,)), ((), ())),
                preferred_element_type=F32,
            )
            total = part if total is None else total + part
        out[...] = (total + before[...]) * factor if last else total

    @pl.when(i < steps)
    def _():
        run(mine, 1)

    @pl.when(i >= steps)
    def _():
        run(other, -1)


def weight_grads(col, ks, mine, other, parts, before, tile, factor):
    n, half = mine[0].shape[2:]
    width = parts[0].shape[-1]
    steps = half // tile
    last = before is not None
    out = pl.BlockSpec(
        (tile, width),
        lambda i, s: (
            jnp.where(i < steps, s[0] * steps + i, (1 - s[0]) * steps + i - steps),
            0,
        ),
    )

    def inputs(start, way):
        def place(i, s):
            return 0, (way * ks[0] % ROWS if last else 0), 0, jnp.clip(i - start, 0, steps - 1)

        return pl.BlockSpec((SIDE, 1 if last else ROWS, n, tile), place)

    return pl.pallas_call(
        functools.partial(weight_body, factor, ks, last),
        grid_spec=pltpu.PrefetchScalarGridSpec(
            num_scalar_prefetch=1,
            grid=(2 * steps,),
            in_specs=[inputs(0, 1)] * SIDE
            + [inputs(steps, -1)] * SIDE
            + [pl.BlockSpec(p.shape, lambda i, s: (0, 0, 0, 0)) for p in parts]
            + ([out] if last else []),
            out_specs=out,
            scratch_shapes=[pltpu.VMEM((len(ks) * SIDE * SIDE * n, width), BF)],
        ),
        out_shape=jax.ShapeDtypeStruct((2 * half, width), F32),
        compiler_params=params(28),
        cost_estimate=FREE,
        name="weight_grads",
    )(col, *mine, *other, *parts, *([before] if last else []))


def shards(inputs, weight, bias, cotangent):
    tok, feats = inputs.shape
    n = tok // ROWS
    width = weight.shape[1] // (SIDE * SIDE)
    r, c, d = lax.axis_index("row"), lax.axis_index("col"), lax.axis_index("depth")
    z, y = d // SIDE, d % SIDE
    way = 1 - 2 * c
    order = [(r - way * k + 2 * ROWS) % ROWS for k in range(ROWS)]
    bias = pltpu.with_memory_space_constraint(bias.reshape(1, -1), pltpu.HBM)
    s0, s1 = [
        jnp.stack(
            [((z + way * kz + SIDE) % SIDE) * 2 + p for kz in chunk for p in range(2)] + order + [c]
        ).astype(jnp.int32)
        for chunk in CHUNKS
    ]
    col = jnp.stack([c]).astype(jnp.int32)
    ys = [(y + way * k + SIDE) % SIDE for k in range(SIDE)]

    def to_column(at, grad, chunk):
        return [
            (grad[j * SIDE : (j + 1) * SIDE] if kz == 0 else at[kz]) for j, kz in enumerate(chunk)
        ]

    def for_y(pieces, k):
        return jnp.stack(
            [lax.dynamic_index_in_dim(p, ys[k], 0, keepdims=False) for p in pieces]
        )

    own0, *send0, token0, x = forward(s0, inputs, weight, width, True)
    got0 = [shift_row(v, -k) for k, v in zip((2, 1, 3), (send0[1], send0[0], send0[2]))]
    x_y1 = shift_y(x, 1)
    own1, *send1, token1 = forward(s1, inputs, weight, width, False, token0)
    got1 = [shift_row(v, -k) for k, v in zip((2, 1, 3), (send1[1], send1[0], send1[2]))]
    x = jnp.concatenate([x, after(x_y1, token1)], axis=0)
    x = jnp.concatenate([x, shift_y(x, 2)], axis=0)
    mine = {1: shift_z(x, 1)}

    grad0, act = gelu(s0, got0, own0, bias, cotangent, None, token1)
    line0 = [grad0, shift_row(grad0, 1)]
    at0 = {
        kz: shift_z(grad0[j * SIDE : (j + 1) * SIDE], kz)
        for j, kz in enumerate(CHUNKS[0])
    }
    grad1, act = gelu(s1, got1, own1, bias, cotangent, act)
    line0.append(shift_row(line0[1], 1))
    line1 = [grad1, shift_row(grad1, 1)]
    at1 = {
        kz: shift_z(grad1[j * SIDE : (j + 1) * SIDE], kz)
        for j, kz in enumerate(CHUNKS[1])
        if kz
    }
    at1 = {kz: after(v, line0[2], mine[1]) for kz, v in at1.items()}
    pieces = to_column(at0, grad0, CHUNKS[0]) + to_column(at1, grad1, CHUNKS[1])
    held = [for_y(pieces, k) for k in range(SIDE)]
    held = [held[0]] + [shift_y(held[k], k) for k in range(1, SIDE)]
    line0.append(shift_row(line0[2], 1))
    line1.append(shift_row(line1[1], 1))
    line1.append(shift_row(line1[2], 1))

    rows = after(jnp.stack(held), line1[2], line0[3])
    near = [shift_row(rows, 1), shift_row(rows, 3)]
    mine[0] = after(x, rows)
    mine[2] = shift_z(mine[0], 2)
    mine[3] = shift_z(mine[0], 3)
    before, token = input_grads(s0, line0, weight, None, rows)
    own_part, other_part, token = input_grads(s1, line1, weight, before)
    mine = {kz: after(v, token) for kz, v in mine.items()}
    other = {kz: swap(mine[kz]) for kz in range(SIDE)}
    cut = SIDE // 2
    far = [
        shift_row(after(near[0][:cut], token), 1),
        shift_row(after(near[1][cut:], token), 3),
    ]
    input_grad = (own_part + swap(other_part)).astype(BF)

    factor = float(tok * lax.axis_size("depth")) ** (-0.5)
    mine = [mine[kz] for kz in range(SIDE)]
    other = [other[kz] for kz in range(SIDE)]
    most = weight_grads(col, (0, 1, 3), mine, other, (rows, *near), None, 256, factor)
    weight_grad = weight_grads(col, (2,), mine, other, far, most, 256, factor)
    return (act, input_grad, weight_grad)


def solution(mesh):
    return jax.shard_map(
        shards,
        mesh=mesh,
        in_specs=(P("depth", "row"), P("row", "col"), P("col"), P(("depth", "row"), "col")),
        out_specs=(
            P(("depth", "row"), "col"),
            P("depth", ("row", "col")),
            P("row", ("col", "depth")),
        ),
        check_vma=False,
    )
```

```python
import functools
import math

import jax
import jax.numpy as jnp
from jax import lax
from jax.experimental import pallas as pl
from jax.experimental.pallas import tpu as pltpu
from jax.sharding import PartitionSpec as P

BF = jnp.bfloat16
F32 = jnp.float32
ROWS, COLS, SIDE = 4, 2, 4
CHUNKS = ((1, 3), (2, 0))
FREE = pl.CostEstimate(flops=0, bytes_accessed=0, transcendentals=0)


def shift(k, along):
    pairs = []
    for c in range(COLS):
        way = k * (1 - 2 * c)
        for at in range(ROWS if along == "row" else SIDE * SIDE):
            z, y = divmod(at, SIDE)
            if along == "row":
                pairs.append((at * COLS + c, (at + way) % ROWS * COLS + c))
            else:
                to = (z + way) % SIDE * SIDE + y if along == "z" else z * SIDE + (y + way) % SIDE
                pairs.append((c * SIDE * SIDE + at, c * SIDE * SIDE + to))
    return pairs


def shift_row(v, k):
    return lax.ppermute(v, ("row", "col"), shift(k, "row"))


def shift_z(v, k):
    return lax.ppermute(v, ("col", "depth"), shift(k, "z"))


def shift_y(v, k):
    return lax.ppermute(v, ("col", "depth"), shift(k, "y"))


def swap(v):
    return lax.ppermute(v, "col", [(0, 1), (1, 0)])


def untouched(*refs):
    pass


def after(v, *earlier):
    anywhere = pl.BlockSpec(memory_space=pl.ANY)
    return pl.pallas_call(
        untouched,
        in_specs=[anywhere] * (1 + len(earlier)),
        out_specs=anywhere,
        out_shape=jax.ShapeDtypeStruct(v.shape, v.dtype),
        input_output_aliases={0: 0},
        compiler_params=params(1),
        cost_estimate=FREE,
        name="after",
    )(v, *earlier)


def waiting(body, count, inputs):
    def inner(*refs):
        return body(*refs[:inputs], *refs[inputs + count :])

    return inner


def params(mib):
    return pltpu.CompilerParams(vmem_limit_bytes=mib << 20)


def forward_body(with_half, s, x, w, own, first, second, third, token, *rest):
    n, width = own.shape[1:]
    steps = pl.num_programs(0)
    rows = rest[-1]

    @pl.when(pl.program_id(0) == 0)
    def _():
        for k in range(ROWS):
            rows[k * n : (k + 1) * n, :] = x[
                pl.ds(pl.multiple_of(s[steps + k] * n, n), n), :
            ]
        if with_half:
            half = x.shape[1] // 2
            at = pl.multiple_of(s[steps + ROWS] * half, half)
            for k in range(ROWS):
                rest[0][0, k] = rows[k * n : (k + 1) * n, pl.ds(at, half)]
        token[...] = jnp.zeros_like(token)

    part = jnp.dot(rows[...], w[...], preferred_element_type=F32)
    for j in range(own.shape[0]):
        cut = part[:, j * width : (j + 1) * width]
        own[j] = cut[:n]
        for k, out in enumerate((first, second, third)):
            out[j] = cut[(k + 1) * n : (k + 2) * n].astype(BF)


TOKEN = jax.ShapeDtypeStruct((8, 128), F32)


def token_spec():
    return pl.BlockSpec((8, 128), lambda i, s: (0, 0))


def forward(scalars, x, w, width, with_half, *earlier):
    count, (tokens, feats) = scalars.shape[0] - ROWS - 1, x.shape
    n = tokens // ROWS
    out = pl.BlockSpec((2, n, width), lambda i, s: (i, 0, 0))
    shape = (2 * count, n, width)
    half = (1, ROWS, n, feats // 2)
    return pl.pallas_call(
        waiting(functools.partial(forward_body, with_half), len(earlier), 3),
        grid_spec=pltpu.PrefetchScalarGridSpec(
            num_scalar_prefetch=1,
            grid=(count,),
            in_specs=[
                pl.BlockSpec((tokens, feats), lambda i, s: (0, 0)),
                pl.BlockSpec((feats, 2 * width), lambda i, s: (0, s[i])),
            ]
            + [pl.BlockSpec(memory_space=pl.ANY)] * len(earlier),
            out_specs=[out] * 4
            + [token_spec()]
            + [pl.BlockSpec(half, lambda i, s: (0, 0, 0, 0))] * with_half,
            scratch_shapes=[pltpu.VMEM((tokens, feats), BF)],
        ),
        out_shape=[jax.ShapeDtypeStruct(shape, d) for d in (F32, BF, BF, BF)]
        + [TOKEN]
        + [jax.ShapeDtypeStruct(half, BF)] * with_half,
        compiler_params=params(20),
        cost_estimate=FREE,
        name="forward",
    )(scalars, x, w, *earlier)


def gelu_body(s, got1, got2, got3, own, bias, cot, *rest):
    grad, act = rest[-2:]
    width = own.shape[2]
    for j in range(own.shape[0]):
        at = slice(j * width, (j + 1) * width)
        pre = got1[j].astype(F32) + got2[j].astype(F32) + got3[j].astype(F32)
        pre = pre + own[j] + bias[:, at]
        cdf = 0.5 * (1.0 + lax.erf(pre / math.sqrt(2.0)))
        dens = jnp.exp(-0.5 * pre * pre) / math.sqrt(2.0 * math.pi)
        act[:, at] = (pre * cdf).astype(BF)
        grad[j] = (cot[:, at].astype(F32) * (cdf + pre * dens)).astype(BF)


def gelu(scalars, got, own, bias, cot, act, *earlier):
    count, n, width = own.shape
    block = pl.BlockSpec((SIDE, n, width), lambda i, s: (i, 0, 0))
    wide = pl.BlockSpec((n, SIDE * width), lambda i, s: (0, s[2 * i] // 2))
    extra = [*([] if act is None else [act]), *earlier]
    return pl.pallas_call(
        gelu_body,
        grid_spec=pltpu.PrefetchScalarGridSpec(
            num_scalar_prefetch=1,
            grid=(count // SIDE,),
            in_specs=[
                block,
                block,
                block,
                block,
                pl.BlockSpec((1, SIDE * width), lambda i, s: (0, s[2 * i] // 2)),
                wide,
            ]
            + [pl.BlockSpec(memory_space=pl.ANY)] * len(extra),
            out_specs=[block, wide],
        ),
        out_shape=[
            jax.ShapeDtypeStruct((count, n, width), BF),
            jax.ShapeDtypeStruct(cot.shape, BF),
        ],
        input_output_aliases={} if act is None else {7: 1},
        compiler_params=params(8),
        cost_estimate=FREE,
        name="gelu",
    )(scalars, *got, own, bias, cot, *extra)


def input_body(last, s, g0, g1, g2, g3, w, *rest):
    i, steps = pl.program_id(0), pl.num_programs(0)
    n = g0.shape[1]
    grad = jnp.concatenate(
        [jnp.concatenate([g[j] for j in range(g.shape[0])], axis=1) for g in (g0, g1, g2, g3)],
        axis=0,
    )
    total, token = rest[-1], rest[-2]
    part = lax.dot_general(
        w[...], grad, (((1,), (1,)), ((), ())), preferred_element_type=F32
    )

    @pl.when(i == 0)
    def _():
        total[...] = part + rest[0][...] if last else part
        token[...] = jnp.zeros_like(token)

    @pl.when(i > 0)
    def _():
        total[...] += part

    @pl.when(i == steps - 1)
    def _():
        if last:
            half = total.shape[0] // 2
            col = s[steps + ROWS]
            for out, h in ((rest[1], col), (rest[2], 1 - col)):
                rows = total[pl.ds(pl.multiple_of(h * half, half), half), :].T
                for k in range(ROWS):
                    place = pl.multiple_of(s[steps + k] * n, n)
                    out[pl.ds(place, n), :] = rows[k * n : (k + 1) * n, :]
        else:
            rest[0][...] = total[...]


def input_grads(scalars, grads, w, before, *earlier):
    count, n, width = grads[0].shape
    feats, last = w.shape[0], before is not None
    tokens = ROWS * n
    block = pl.BlockSpec((2, n, width), lambda i, s: (i, 0, 0))
    acc = (feats, tokens)
    whole = pl.BlockSpec(acc, lambda i, s: (0, 0))
    shape = (tokens, feats // 2)
    one = pl.BlockSpec(shape, lambda i, s: (0, 0))
    return pl.pallas_call(
        waiting(functools.partial(input_body, last), len(earlier), 7 if last else 6),
        grid_spec=pltpu.PrefetchScalarGridSpec(
            num_scalar_prefetch=1,
            grid=(count // 2,),
            in_specs=[block] * 4
            + [pl.BlockSpec((feats, 2 * width), lambda i, s: (0, s[i]))]
            + ([whole] if last else [])
            + [pl.BlockSpec(memory_space=pl.ANY)] * len(earlier),
            out_specs=([one, one] if last else [whole]) + [token_spec()],
            scratch_shapes=[pltpu.VMEM(acc, F32)],
        ),
        out_shape=(
            [jax.ShapeDtypeStruct(shape, F32)] * 2
            if last
            else [jax.ShapeDtypeStruct(acc, F32)]
        )
        + [TOKEN],
        compiler_params=params(24),
        cost_estimate=FREE,
        name="input_grads",
    )(scalars, *grads, w, *([before] if last else []), *earlier)


KZS = tuple(kz for chunk in CHUNKS for kz in chunk)


def weight_body(factor, ks, last, col, *refs):
    mine, other, refs = refs[:SIDE], refs[SIDE : 2 * SIDE], refs[2 * SIDE :]
    parts, before, out, rhs = refs[: -2 - last], refs[-2 - last], refs[-2], refs[-1]
    i, steps = pl.program_id(0), pl.num_programs(0) // 2
    n = parts[0].shape[2]
    rows = SIDE * SIDE * n

    @pl.when(i == 0)
    def _():
        at = 0
        for part in parts:
            for ky in range(part.shape[0]):
                for spot in range(SIDE):
                    rhs[at : at + n, :] = part[ky, spot]
                    at += n

    def run(x, way):
        total = None
        for j, k in enumerate(ks):
            lhs = jnp.concatenate(
                [
                    x[way * kz % SIDE][way * ky % SIDE, 0 if last else way * k % ROWS]
                    for ky in range(SIDE)
                    for kz in KZS
                ],
                axis=0,
            )
            part = lax.dot_general(
                lhs,
                rhs[j * rows : (j + 1) * rows, :],
                (((0,), (0,)), ((), ())),
                preferred_element_type=F32,
            )
            total = part if total is None else total + part
        out[...] = (total + before[...]) * factor if last else total

    @pl.when(i < steps)
    def _():
        run(mine, 1)

    @pl.when(i >= steps)
    def _():
        run(other, -1)


def weight_grads(col, ks, mine, other, parts, before, tile, factor):
    n, half = mine[0].shape[2:]
    width = parts[0].shape[-1]
    steps = half // tile
    last = before is not None
    out = pl.BlockSpec(
        (tile, width),
        lambda i, s: (
            jnp.where(i < steps, s[0] * steps + i, (1 - s[0]) * steps + i - steps),
            0,
        ),
    )

    def inputs(start, way):
        def place(i, s):
            return 0, (way * ks[0] % ROWS if last else 0), 0, jnp.clip(i - start, 0, steps - 1)

        return pl.BlockSpec((SIDE, 1 if last else ROWS, n, tile), place)

    return pl.pallas_call(
        functools.partial(weight_body, factor, ks, last),
        grid_spec=pltpu.PrefetchScalarGridSpec(
            num_scalar_prefetch=1,
            grid=(2 * steps,),
            in_specs=[inputs(0, 1)] * SIDE
            + [inputs(steps, -1)] * SIDE
            + [pl.BlockSpec(p.shape, lambda i, s: (0, 0, 0, 0)) for p in parts]
            + ([out] if last else []),
            out_specs=out,
            scratch_shapes=[pltpu.VMEM((len(ks) * SIDE * SIDE * n, width), BF)],
        ),
        out_shape=(jax.ShapeDtypeStruct if last else pltpu.VMEM)((2 * half, width), F32),
        compiler_params=params(28),
        cost_estimate=FREE,
        name="weight_grads",
    )(col, *mine, *other, *parts, *([before] if last else []))


def shards(inputs, weight, bias, cotangent):
    tok, feats = inputs.shape
    n = tok // ROWS
    width = weight.shape[1] // (SIDE * SIDE)
    r, c, d = lax.axis_index("row"), lax.axis_index("col"), lax.axis_index("depth")
    z, y = d // SIDE, d % SIDE
    way = 1 - 2 * c
    order = [(r - way * k + 2 * ROWS) % ROWS for k in range(ROWS)]
    inputs = pltpu.with_memory_space_constraint(inputs, pltpu.HBM)
    bias = pltpu.with_memory_space_constraint(bias.reshape(1, -1), pltpu.HBM)
    s0, s1 = [
        jnp.stack(
            [((z + way * kz + SIDE) % SIDE) * 2 + p for kz in chunk for p in range(2)] + order + [c]
        ).astype(jnp.int32)
        for chunk in CHUNKS
    ]
    col = jnp.stack([c]).astype(jnp.int32)
    ys = [(y + way * k + SIDE) % SIDE for k in range(SIDE)]

    def to_column(at, grad, chunk):
        return [
            (grad[j * SIDE : (j + 1) * SIDE] if kz == 0 else at[kz]) for j, kz in enumerate(chunk)
        ]

    def for_y(pieces, k):
        return jnp.stack(
            [lax.dynamic_index_in_dim(p, ys[k], 0, keepdims=False) for p in pieces]
        )

    own0, *send0, token0, x = forward(s0, inputs, weight, width, True)
    got0 = [shift_row(send0[k - 1], -k) for k in (2, 1, 3)]
    x_y1 = shift_y(x, 1)
    own1, *send1, token1 = forward(s1, inputs, weight, width, False, token0)
    got1 = [shift_row(send1[k - 1], -k) for k in (2, 1, 3)]
    x = jnp.concatenate([x, after(x_y1, token1)], axis=0)
    x = jnp.concatenate([x, shift_y(x, 2)], axis=0)
    mine = {1: shift_z(x, 1)}

    grad0, act = gelu(s0, got0, own0, bias, cotangent, None, token1)
    line0 = [grad0, shift_row(grad0, 1)]
    at0 = {kz: shift_z(grad0[j * SIDE : (j + 1) * SIDE], kz) for j, kz in enumerate(CHUNKS[0])}
    grad1, act = gelu(s1, got1, own1, bias, cotangent, act)
    line0.append(shift_row(line0[1], 1))
    line1 = [grad1, shift_row(grad1, 1)]
    at1 = {
        kz: shift_z(grad1[j * SIDE : (j + 1) * SIDE], kz)
        for j, kz in enumerate(CHUNKS[1])
        if kz
    }
    at1 = {kz: after(v, line0[2]) for kz, v in at1.items()}
    pieces = to_column(at0, grad0, CHUNKS[0]) + to_column(at1, grad1, CHUNKS[1])
    held = [for_y(pieces, k) for k in range(SIDE)]
    held = [held[0]] + [shift_y(held[k], k) for k in range(1, SIDE)]
    line0.append(shift_row(line0[2], 1))
    line1.append(shift_row(line1[1], 1))
    line1.append(shift_row(line1[2], 1))

    rows = after(jnp.stack(held), line1[2], line0[3])
    near = [shift_row(rows, 1), shift_row(rows, 3)]
    mine[0] = after(x, *at1.values())
    mine[2] = shift_z(mine[0], 2)
    mine[3] = shift_z(mine[0], 3)
    before, token = input_grads(s0, line0, weight, None, rows)
    own_part, other_part, token = input_grads(s1, line1, weight, before)
    mine = {kz: after(v, token) for kz, v in mine.items()}
    other = {kz: swap(mine[kz]) for kz in range(SIDE)}
    cut = SIDE // 2
    far = [
        shift_row(after(near[0][:cut], token), 1),
        shift_row(after(near[1][cut:], token), 3),
    ]
    input_grad = (own_part + swap(other_part)).astype(BF)

    factor = float(tok * lax.axis_size("depth")) ** (-0.5)
    mine = [mine[kz] for kz in range(SIDE)]
    other = [other[kz] for kz in range(SIDE)]
    most = weight_grads(col, (0, 1, 3), mine, other, (rows, *near), None, 384, factor)
    weight_grad = weight_grads(col, (2,), mine, other, far, most, 384, factor)
    return (act, input_grad, weight_grad)


def solution(mesh):
    return jax.shard_map(
        shards,
        mesh=mesh,
        in_specs=(P("depth", "row"), P("row", "col"), P("col"), P(("depth", "row"), "col")),
        out_specs=(
            P(("depth", "row"), "col"),
            P("depth", ("row", "col")),
            P("row", ("col", "depth")),
        ),
        check_vma=False,
    )
```

```python
import functools
import math

import jax
import jax.numpy as jnp
from jax import lax
from jax.experimental import pallas as pl
from jax.experimental.pallas import tpu as pltpu
from jax.sharding import PartitionSpec as P

BF = jnp.bfloat16
F32 = jnp.float32
ROWS, COLS, SIDE = 4, 2, 4
CHUNKS = ((1, 3), (2, 0))
FREE = pl.CostEstimate(flops=0, bytes_accessed=0, transcendentals=0)


def shift(k, along):
    pairs = []
    for c in range(COLS):
        way = k * (1 - 2 * c)
        for at in range(ROWS if along == "row" else SIDE * SIDE):
            z, y = divmod(at, SIDE)
            if along == "row":
                pairs.append((at * COLS + c, (at + way) % ROWS * COLS + c))
            else:
                to = (z + way) % SIDE * SIDE + y if along == "z" else z * SIDE + (y + way) % SIDE
                pairs.append((c * SIDE * SIDE + at, c * SIDE * SIDE + to))
    return pairs


def shift_row(v, k):
    return lax.ppermute(v, ("row", "col"), shift(k, "row"))


def shift_z(v, k):
    return lax.ppermute(v, ("col", "depth"), shift(k, "z"))


def shift_y(v, k):
    return lax.ppermute(v, ("col", "depth"), shift(k, "y"))


def swap(v):
    return lax.ppermute(v, "col", [(0, 1), (1, 0)])


def untouched(*refs):
    pass


def after(v, *earlier):
    anywhere = pl.BlockSpec(memory_space=pl.ANY)
    return pl.pallas_call(
        untouched,
        in_specs=[anywhere] * (1 + len(earlier)),
        out_specs=anywhere,
        out_shape=jax.ShapeDtypeStruct(v.shape, v.dtype),
        input_output_aliases={0: 0},
        compiler_params=params(1),
        cost_estimate=FREE,
        name="after",
    )(v, *earlier)


def waiting(body, count, inputs):
    def inner(*refs):
        return body(*refs[:inputs], *refs[inputs + count :])

    return inner


def params(mib):
    return pltpu.CompilerParams(vmem_limit_bytes=mib << 20)


def forward_body(with_half, s, x, w, own, first, second, third, token, *rest):
    n, width = own.shape[1:]
    steps = pl.num_programs(0)
    rows = rest[-1]

    @pl.when(pl.program_id(0) == 0)
    def _():
        for k in range(ROWS):
            rows[k * n : (k + 1) * n, :] = x[
                pl.ds(pl.multiple_of(s[steps + k] * n, n), n), :
            ]
        if with_half:
            half = x.shape[1] // 2
            at = pl.multiple_of(s[steps + ROWS] * half, half)
            for k in range(ROWS):
                rest[0][0, k] = rows[k * n : (k + 1) * n, pl.ds(at, half)]
        token[...] = jnp.zeros_like(token)

    part = jnp.dot(rows[...], w[...], preferred_element_type=F32)
    for j in range(own.shape[0]):
        cut = part[:, j * width : (j + 1) * width]
        own[j] = cut[:n]
        for k, out in enumerate((first, second, third)):
            out[j] = cut[(k + 1) * n : (k + 2) * n].astype(BF)


TOKEN = jax.ShapeDtypeStruct((8, 128), F32)


def token_spec():
    return pl.BlockSpec((8, 128), lambda i, s: (0, 0))


def forward(scalars, x, w, width, with_half, *earlier):
    count, (tokens, feats) = scalars.shape[0] - ROWS - 1, x.shape
    n = tokens // ROWS
    out = pl.BlockSpec((2, n, width), lambda i, s: (i, 0, 0))
    shape = (2 * count, n, width)
    half = (1, ROWS, n, feats // 2)
    return pl.pallas_call(
        waiting(functools.partial(forward_body, with_half), len(earlier), 3),
        grid_spec=pltpu.PrefetchScalarGridSpec(
            num_scalar_prefetch=1,
            grid=(count,),
            in_specs=[
                pl.BlockSpec((tokens, feats), lambda i, s: (0, 0)),
                pl.BlockSpec((feats, 2 * width), lambda i, s: (0, s[i])),
            ]
            + [pl.BlockSpec(memory_space=pl.ANY)] * len(earlier),
            out_specs=[out] * 4
            + [token_spec()]
            + [pl.BlockSpec(half, lambda i, s: (0, 0, 0, 0))] * with_half,
            scratch_shapes=[pltpu.VMEM((tokens, feats), BF)],
        ),
        out_shape=[jax.ShapeDtypeStruct(shape, d) for d in (F32, BF, BF, BF)]
        + [TOKEN]
        + [jax.ShapeDtypeStruct(half, BF)] * with_half,
        compiler_params=params(20),
        cost_estimate=FREE,
        name="forward",
    )(scalars, x, w, *earlier)


def gelu_body(s, got1, got2, got3, own, bias, cot, *rest):
    grad, act = rest[-2:]
    width = own.shape[2]
    for j in range(own.shape[0]):
        at = slice(j * width, (j + 1) * width)
        pre = got1[j].astype(F32) + got2[j].astype(F32) + got3[j].astype(F32)
        pre = pre + own[j] + bias[:, at]
        cdf = 0.5 * (1.0 + lax.erf(pre / math.sqrt(2.0)))
        dens = jnp.exp(-0.5 * pre * pre) / math.sqrt(2.0 * math.pi)
        act[:, at] = (pre * cdf).astype(BF)
        grad[j] = (cot[:, at].astype(F32) * (cdf + pre * dens)).astype(BF)


def gelu(scalars, got, own, bias, cot, act, *earlier):
    count, n, width = own.shape
    block = pl.BlockSpec((SIDE, n, width), lambda i, s: (i, 0, 0))
    wide = pl.BlockSpec((n, SIDE * width), lambda i, s: (0, s[2 * i] // 2))
    extra = [*([] if act is None else [act]), *earlier]
    return pl.pallas_call(
        gelu_body,
        grid_spec=pltpu.PrefetchScalarGridSpec(
            num_scalar_prefetch=1,
            grid=(count // SIDE,),
            in_specs=[
                block,
                block,
                block,
                block,
                pl.BlockSpec((1, SIDE * width), lambda i, s: (0, s[2 * i] // 2)),
                wide,
            ]
            + [pl.BlockSpec(memory_space=pl.ANY)] * len(extra),
            out_specs=[block, wide],
        ),
        out_shape=[
            jax.ShapeDtypeStruct((count, n, width), BF),
            jax.ShapeDtypeStruct(cot.shape, BF),
        ],
        input_output_aliases={} if act is None else {7: 1},
        compiler_params=params(8),
        cost_estimate=FREE,
        name="gelu",
    )(scalars, *got, own, bias, cot, *extra)


def input_body(last, s, g0, g1, g2, g3, w, *rest):
    i, steps = pl.program_id(0), pl.num_programs(0)
    n = g0.shape[1]
    grad = jnp.concatenate(
        [jnp.concatenate([g[j] for j in range(g.shape[0])], axis=1) for g in (g0, g1, g2, g3)],
        axis=0,
    )
    total, token = rest[-1], rest[-2]
    part = lax.dot_general(
        w[...], grad, (((1,), (1,)), ((), ())), preferred_element_type=F32
    )

    @pl.when(i == 0)
    def _():
        total[...] = part + rest[0][...] if last else part
        token[...] = jnp.zeros_like(token)

    @pl.when(i > 0)
    def _():
        total[...] += part

    @pl.when(i == steps - 1)
    def _():
        if last:
            half = total.shape[0] // 2
            col = s[steps + ROWS]
            for out, h in ((rest[1], col), (rest[2], 1 - col)):
                rows = total[pl.ds(pl.multiple_of(h * half, half), half), :].T
                for k in range(ROWS):
                    place = pl.multiple_of(s[steps + k] * n, n)
                    out[pl.ds(place, n), :] = rows[k * n : (k + 1) * n, :]
        else:
            rest[0][...] = total[...]


def input_grads(scalars, grads, w, before, *earlier):
    count, n, width = grads[0].shape
    feats, last = w.shape[0], before is not None
    tokens = ROWS * n
    block = pl.BlockSpec((2, n, width), lambda i, s: (i, 0, 0))
    acc = (feats, tokens)
    whole = pl.BlockSpec(acc, lambda i, s: (0, 0))
    shape = (tokens, feats // 2)
    one = pl.BlockSpec(shape, lambda i, s: (0, 0))
    return pl.pallas_call(
        waiting(functools.partial(input_body, last), len(earlier), 7 if last else 6),
        grid_spec=pltpu.PrefetchScalarGridSpec(
            num_scalar_prefetch=1,
            grid=(count // 2,),
            in_specs=[block] * 4
            + [pl.BlockSpec((feats, 2 * width), lambda i, s: (0, s[i]))]
            + ([whole] if last else [])
            + [pl.BlockSpec(memory_space=pl.ANY)] * len(earlier),
            out_specs=([one, one] if last else [whole]) + [token_spec()],
            scratch_shapes=[pltpu.VMEM(acc, F32)],
        ),
        out_shape=(
            [jax.ShapeDtypeStruct(shape, F32)] * 2
            if last
            else [jax.ShapeDtypeStruct(acc, F32)]
        )
        + [TOKEN],
        compiler_params=params(24),
        cost_estimate=FREE,
        name="input_grads",
    )(scalars, *grads, w, *([before] if last else []), *earlier)


KZS = tuple(kz for chunk in CHUNKS for kz in chunk)


def weight_body(factor, ks, last, col, *refs):
    mine, other, refs = refs[:SIDE], refs[SIDE : 2 * SIDE], refs[2 * SIDE :]
    parts, before, out, rhs = refs[: -2 - last], refs[-2 - last], refs[-2], refs[-1]
    i, steps = pl.program_id(0), pl.num_programs(0) // 2
    n = parts[0].shape[2]
    rows = SIDE * SIDE * n

    @pl.when(i == 0)
    def _():
        at = 0
        for part in parts:
            for ky in range(part.shape[0]):
                for spot in range(SIDE):
                    rhs[at : at + n, :] = part[ky, spot]
                    at += n

    def run(x, way):
        total = None
        for j, k in enumerate(ks):
            lhs = jnp.concatenate(
                [
                    x[way * kz % SIDE][way * ky % SIDE, 0 if last else way * k % ROWS]
                    for ky in range(SIDE)
                    for kz in KZS
                ],
                axis=0,
            )
            part = lax.dot_general(
                lhs,
                rhs[j * rows : (j + 1) * rows, :],
                (((0,), (0,)), ((), ())),
                preferred_element_type=F32,
            )
            total = part if total is None else total + part
        out[...] = (total + before[...]) * factor if last else total

    @pl.when(i < steps)
    def _():
        run(mine, 1)

    @pl.when(i >= steps)
    def _():
        run(other, -1)


def weight_grads(col, ks, mine, other, parts, before, tile, factor):
    n, half = mine[0].shape[2:]
    width = parts[0].shape[-1]
    steps = half // tile
    last = before is not None
    out = pl.BlockSpec(
        (tile, width),
        lambda i, s: (
            jnp.where(i < steps, s[0] * steps + i, (1 - s[0]) * steps + i - steps),
            0,
        ),
    )

    def inputs(start, way):
        def place(i, s):
            return 0, (way * ks[0] % ROWS if last else 0), 0, jnp.clip(i - start, 0, steps - 1)

        return pl.BlockSpec((SIDE, 1 if last else ROWS, n, tile), place)

    return pl.pallas_call(
        functools.partial(weight_body, factor, ks, last),
        grid_spec=pltpu.PrefetchScalarGridSpec(
            num_scalar_prefetch=1,
            grid=(2 * steps,),
            in_specs=[inputs(0, 1)] * SIDE
            + [inputs(steps, -1)] * SIDE
            + [pl.BlockSpec(p.shape, lambda i, s: (0, 0, 0, 0)) for p in parts]
            + ([out] if last else []),
            out_specs=out,
            scratch_shapes=[pltpu.VMEM((len(ks) * SIDE * SIDE * n, width), BF)],
        ),
        out_shape=(jax.ShapeDtypeStruct if last else pltpu.VMEM)((2 * half, width), F32),
        compiler_params=params(28),
        cost_estimate=FREE,
        name="weight_grads",
    )(col, *mine, *other, *parts, *([before] if last else []))


def shards(inputs, weight, bias, cotangent):
    tok, feats = inputs.shape
    n = tok // ROWS
    width = weight.shape[1] // (SIDE * SIDE)
    r, c, d = lax.axis_index("row"), lax.axis_index("col"), lax.axis_index("depth")
    z, y = d // SIDE, d % SIDE
    way = 1 - 2 * c
    order = [(r - way * k + 2 * ROWS) % ROWS for k in range(ROWS)]
    inputs = pltpu.with_memory_space_constraint(inputs, pltpu.HBM)
    bias = pltpu.with_memory_space_constraint(bias.reshape(1, -1), pltpu.HBM)
    s0, s1 = [
        jnp.stack(
            [((z + way * kz + SIDE) % SIDE) * 2 + p for kz in chunk for p in range(2)] + order + [c]
        ).astype(jnp.int32)
        for chunk in CHUNKS
    ]
    col = jnp.stack([c]).astype(jnp.int32)
    ys = [(y + way * k + SIDE) % SIDE for k in range(SIDE)]

    def to_column(at, grad, chunk):
        return [
            (grad[j * SIDE : (j + 1) * SIDE] if kz == 0 else at[kz]) for j, kz in enumerate(chunk)
        ]

    def for_y(pieces, k):
        return jnp.stack(
            [lax.dynamic_index_in_dim(p, ys[k], 0, keepdims=False) for p in pieces]
        )

    own0, *send0, token0, x = forward(s0, inputs, weight, width, True)
    got0 = [shift_row(send0[k - 1], -k) for k in (2, 1, 3)]
    x_y1 = shift_y(x, 1)
    own1, *send1, token1 = forward(s1, inputs, weight, width, False, token0)
    got1 = [shift_row(send1[k - 1], -k) for k in (2, 1, 3)]
    x = jnp.concatenate([x, after(x_y1, token1)], axis=0)
    x = jnp.concatenate([x, shift_y(x, 2)], axis=0)
    mine = {1: shift_z(x, 1)}

    grad0, act = gelu(s0, got0, own0, bias, cotangent, None, token1)
    line0 = [grad0, shift_row(grad0, 1)]
    at0 = {kz: shift_z(grad0[j * SIDE : (j + 1) * SIDE], kz) for j, kz in enumerate(CHUNKS[0])}
    grad1, act = gelu(s1, got1, own1, bias, cotangent, act)
    line0.append(shift_row(line0[1], 1))
    line1 = [grad1, shift_row(grad1, 1)]
    at1 = {
        kz: shift_z(grad1[j * SIDE : (j + 1) * SIDE], kz)
        for j, kz in enumerate(CHUNKS[1])
        if kz
    }
    at1 = {kz: after(v, line0[2]) for kz, v in at1.items()}
    pieces = to_column(at0, grad0, CHUNKS[0]) + to_column(at1, grad1, CHUNKS[1])
    held = [for_y(pieces, k) for k in range(SIDE)]
    held = [held[0]] + [shift_y(held[k], k) for k in range(1, SIDE)]
    line0.append(shift_row(line0[2], 1))
    line1.append(shift_row(line1[1], 1))
    line1.append(shift_row(line1[2], 1))

    rows = jnp.stack(held)
    near = [shift_row(rows, 1), shift_row(rows, 3)]
    mine[0] = after(x, *at1.values())
    mine[2] = shift_z(mine[0], 2)
    mine[3] = shift_z(mine[0], 3)
    before, token = input_grads(s0, line0, weight, None, rows)
    own_part, other_part, token = input_grads(s1, line1, weight, before)
    mine = {kz: after(v, token) for kz, v in mine.items()}
    other = {kz: swap(mine[kz]) for kz in range(SIDE)}
    cut = SIDE // 2
    far = [
        shift_row(after(near[0][:cut], token), 1),
        shift_row(after(near[1][cut:], token), 3),
    ]
    input_grad = (own_part + swap(other_part)).astype(BF)

    factor = float(tok * lax.axis_size("depth")) ** (-0.5)
    mine = [mine[kz] for kz in range(SIDE)]
    other = [other[kz] for kz in range(SIDE)]
    most = weight_grads(col, (0, 1, 3), mine, other, (rows, *near), None, 384, factor)
    weight_grad = weight_grads(col, (2,), mine, other, far, most, 384, factor)
    return (act, input_grad, weight_grad)


def solution(mesh):
    return jax.shard_map(
        shards,
        mesh=mesh,
        in_specs=(P("depth", "row"), P("row", "col"), P("col"), P(("depth", "row"), "col")),
        out_specs=(
            P(("depth", "row"), "col"),
            P("depth", ("row", "col")),
            P("row", ("col", "depth")),
        ),
        check_vma=False,
    )
```

```python
import functools
import math

import jax
import jax.numpy as jnp
from jax import lax
from jax.experimental import pallas as pl
from jax.experimental.pallas import tpu as pltpu
from jax.sharding import PartitionSpec as P

BF = jnp.bfloat16
F32 = jnp.float32
ROWS, COLS, SIDE = 4, 2, 4
CHUNKS = ((1, 3), (2, 0))
FREE = pl.CostEstimate(flops=0, bytes_accessed=0, transcendentals=0)


def shift(k, along):
    pairs = []
    for c in range(COLS):
        way = k * (1 - 2 * c)
        for at in range(ROWS if along == "row" else SIDE * SIDE):
            z, y = divmod(at, SIDE)
            if along == "row":
                pairs.append((at * COLS + c, (at + way) % ROWS * COLS + c))
            else:
                to = (z + way) % SIDE * SIDE + y if along == "z" else z * SIDE + (y + way) % SIDE
                pairs.append((c * SIDE * SIDE + at, c * SIDE * SIDE + to))
    return pairs


def shift_row(v, k):
    return lax.ppermute(v, ("row", "col"), shift(k, "row"))


def shift_z(v, k):
    return lax.ppermute(v, ("col", "depth"), shift(k, "z"))


def shift_y(v, k):
    return lax.ppermute(v, ("col", "depth"), shift(k, "y"))


def swap(v):
    return lax.ppermute(v, "col", [(0, 1), (1, 0)])


def untouched(*refs):
    pass


def after(v, *earlier):
    anywhere = pl.BlockSpec(memory_space=pl.ANY)
    return pl.pallas_call(
        untouched,
        in_specs=[anywhere] * (1 + len(earlier)),
        out_specs=anywhere,
        out_shape=jax.ShapeDtypeStruct(v.shape, v.dtype),
        input_output_aliases={0: 0},
        compiler_params=params(1),
        cost_estimate=FREE,
        name="after",
    )(v, *earlier)


def waiting(body, count, inputs):
    def inner(*refs):
        return body(*refs[:inputs], *refs[inputs + count :])

    return inner


def params(mib):
    return pltpu.CompilerParams(vmem_limit_bytes=mib << 20)


def forward_body(with_half, s, x, w, own, first, second, third, token, *rest):
    n, width = own.shape[1:]
    steps = pl.num_programs(0)
    rows = rest[-1]

    @pl.when(pl.program_id(0) == 0)
    def _():
        for k in range(ROWS):
            rows[k * n : (k + 1) * n, :] = x[
                pl.ds(pl.multiple_of(s[steps + k] * n, n), n), :
            ]
        if with_half:
            half = x.shape[1] // 2
            at = pl.multiple_of(s[steps + ROWS] * half, half)
            for k in range(ROWS):
                rest[0][0, k] = rows[k * n : (k + 1) * n, pl.ds(at, half)]
        token[...] = jnp.zeros_like(token)

    part = jnp.dot(rows[...], w[...], preferred_element_type=F32)
    for j in range(own.shape[0]):
        cut = part[:, j * width : (j + 1) * width]
        own[j] = cut[:n]
        for k, out in enumerate((first, second, third)):
            out[j] = cut[(k + 1) * n : (k + 2) * n].astype(BF)


TOKEN = jax.ShapeDtypeStruct((8, 128), F32)


def token_spec():
    return pl.BlockSpec((8, 128), lambda i, s: (0, 0))


def forward(scalars, x, w, width, with_half, *earlier):
    count, (tokens, feats) = scalars.shape[0] - ROWS - 1, x.shape
    n = tokens // ROWS
    out = pl.BlockSpec((2, n, width), lambda i, s: (i, 0, 0))
    shape = (2 * count, n, width)
    half = (1, ROWS, n, feats // 2)
    return pl.pallas_call(
        waiting(functools.partial(forward_body, with_half), len(earlier), 3),
        grid_spec=pltpu.PrefetchScalarGridSpec(
            num_scalar_prefetch=1,
            grid=(count,),
            in_specs=[
                pl.BlockSpec((tokens, feats), lambda i, s: (0, 0)),
                pl.BlockSpec((feats, 2 * width), lambda i, s: (0, s[i])),
            ]
            + [pl.BlockSpec(memory_space=pl.ANY)] * len(earlier),
            out_specs=[out] * 4
            + [token_spec()]
            + [pl.BlockSpec(half, lambda i, s: (0, 0, 0, 0))] * with_half,
            scratch_shapes=[pltpu.VMEM((tokens, feats), BF)],
        ),
        out_shape=[jax.ShapeDtypeStruct(shape, d) for d in (F32, BF, BF, BF)]
        + [TOKEN]
        + [jax.ShapeDtypeStruct(half, BF)] * with_half,
        compiler_params=params(20),
        cost_estimate=FREE,
        name="forward",
    )(scalars, x, w, *earlier)


def gelu_body(s, got1, got2, got3, own, bias, cot, *rest):
    grad, act = rest[-2:]
    width = own.shape[2]
    for j in range(own.shape[0]):
        at = slice(j * width, (j + 1) * width)
        pre = got1[j].astype(F32) + got2[j].astype(F32) + got3[j].astype(F32)
        pre = pre + own[j] + bias[:, at]
        cdf = 0.5 * (1.0 + lax.erf(pre / math.sqrt(2.0)))
        dens = jnp.exp(-0.5 * pre * pre) / math.sqrt(2.0 * math.pi)
        act[:, at] = (pre * cdf).astype(BF)
        grad[j] = (cot[:, at].astype(F32) * (cdf + pre * dens)).astype(BF)


def gelu(scalars, got, own, bias, cot, act, *earlier):
    count, n, width = own.shape
    block = pl.BlockSpec((SIDE, n, width), lambda i, s: (i, 0, 0))
    wide = pl.BlockSpec((n, SIDE * width), lambda i, s: (0, s[2 * i] // 2))
    extra = [*([] if act is None else [act]), *earlier]
    return pl.pallas_call(
        gelu_body,
        grid_spec=pltpu.PrefetchScalarGridSpec(
            num_scalar_prefetch=1,
            grid=(count // SIDE,),
            in_specs=[
                block,
                block,
                block,
                block,
                pl.BlockSpec((1, SIDE * width), lambda i, s: (0, s[2 * i] // 2)),
                wide,
            ]
            + [pl.BlockSpec(memory_space=pl.ANY)] * len(extra),
            out_specs=[block, wide],
        ),
        out_shape=[
            jax.ShapeDtypeStruct((count, n, width), BF),
            jax.ShapeDtypeStruct(cot.shape, BF),
        ],
        input_output_aliases={} if act is None else {7: 1},
        compiler_params=params(8),
        cost_estimate=FREE,
        name="gelu",
    )(scalars, *got, own, bias, cot, *extra)


def input_body(last, s, g0, g1, g2, g3, w, *rest):
    i, steps = pl.program_id(0), pl.num_programs(0)
    n = g0.shape[1]
    grad = jnp.concatenate(
        [jnp.concatenate([g[j] for j in range(g.shape[0])], axis=1) for g in (g0, g1, g2, g3)],
        axis=0,
    )
    total, token = rest[-1], rest[-2]
    part = lax.dot_general(
        w[...], grad, (((1,), (1,)), ((), ())), preferred_element_type=F32
    )

    @pl.when(i == 0)
    def _():
        total[...] = part + rest[0][...] if last else part
        token[...] = jnp.zeros_like(token)

    @pl.when(i > 0)
    def _():
        total[...] += part

    @pl.when(i == steps - 1)
    def _():
        if last:
            half = total.shape[0] // 2
            col = s[steps + ROWS]
            for out, h in ((rest[1], col), (rest[2], 1 - col)):
                rows = total[pl.ds(pl.multiple_of(h * half, half), half), :].T
                for k in range(ROWS):
                    place = pl.multiple_of(s[steps + k] * n, n)
                    out[pl.ds(place, n), :] = rows[k * n : (k + 1) * n, :]
        else:
            rest[0][...] = total[...]


def input_grads(scalars, grads, w, before, *earlier):
    count, n, width = grads[0].shape
    feats, last = w.shape[0], before is not None
    tokens = ROWS * n
    block = pl.BlockSpec((2, n, width), lambda i, s: (i, 0, 0))
    acc = (feats, tokens)
    whole = pl.BlockSpec(acc, lambda i, s: (0, 0))
    shape = (tokens, feats // 2)
    one = pl.BlockSpec(shape, lambda i, s: (0, 0))
    return pl.pallas_call(
        waiting(functools.partial(input_body, last), len(earlier), 7 if last else 6),
        grid_spec=pltpu.PrefetchScalarGridSpec(
            num_scalar_prefetch=1,
            grid=(count // 2,),
            in_specs=[block] * 4
            + [pl.BlockSpec((feats, 2 * width), lambda i, s: (0, s[i]))]
            + ([whole] if last else [])
            + [pl.BlockSpec(memory_space=pl.ANY)] * len(earlier),
            out_specs=([one, one] if last else [whole]) + [token_spec()],
            scratch_shapes=[pltpu.VMEM(acc, F32)],
        ),
        out_shape=(
            [jax.ShapeDtypeStruct(shape, F32)] * 2
            if last
            else [jax.ShapeDtypeStruct(acc, F32)]
        )
        + [TOKEN],
        compiler_params=params(24),
        cost_estimate=FREE,
        name="input_grads",
    )(scalars, *grads, w, *([before] if last else []), *earlier)


KZS = tuple(kz for chunk in CHUNKS for kz in chunk)


def weight_body(factor, ks, last, col, *refs):
    mine, other, refs = refs[:SIDE], refs[SIDE : 2 * SIDE], refs[2 * SIDE :]
    parts, before, out, rhs = refs[: -2 - last], refs[-2 - last], refs[-2], refs[-1]
    i, steps = pl.program_id(0), pl.num_programs(0) // 2
    n = parts[0].shape[2]
    rows = SIDE * SIDE * n

    @pl.when(i == 0)
    def _():
        at = 0
        for part in parts:
            for ky in range(part.shape[0]):
                for spot in range(SIDE):
                    rhs[at : at + n, :] = part[ky, spot]
                    at += n

    def run(x, way):
        total = None
        for j, k in enumerate(ks):
            lhs = jnp.concatenate(
                [
                    x[way * kz % SIDE][way * ky % SIDE, 0 if last else way * k % ROWS]
                    for ky in range(SIDE)
                    for kz in KZS
                ],
                axis=0,
            )
            part = lax.dot_general(
                lhs,
                rhs[j * rows : (j + 1) * rows, :],
                (((0,), (0,)), ((), ())),
                preferred_element_type=F32,
            )
            total = part if total is None else total + part
        out[...] = (total + before[...]) * factor if last else total

    @pl.when(i < steps)
    def _():
        run(mine, 1)

    @pl.when(i >= steps)
    def _():
        run(other, -1)


def weight_grads(col, ks, mine, other, parts, before, tile, factor):
    n, half = mine[0].shape[2:]
    width = parts[0].shape[-1]
    steps = half // tile
    last = before is not None
    out = pl.BlockSpec(
        (tile, width),
        lambda i, s: (
            jnp.where(i < steps, s[0] * steps + i, (1 - s[0]) * steps + i - steps),
            0,
        ),
    )

    def inputs(start, way):
        def place(i, s):
            return 0, (way * ks[0] % ROWS if last else 0), 0, jnp.clip(i - start, 0, steps - 1)

        return pl.BlockSpec((SIDE, 1 if last else ROWS, n, tile), place)

    return pl.pallas_call(
        functools.partial(weight_body, factor, ks, last),
        grid_spec=pltpu.PrefetchScalarGridSpec(
            num_scalar_prefetch=1,
            grid=(2 * steps,),
            in_specs=[inputs(0, 1)] * SIDE
            + [inputs(steps, -1)] * SIDE
            + [pl.BlockSpec(p.shape, lambda i, s: (0, 0, 0, 0)) for p in parts]
            + ([out] if last else []),
            out_specs=out,
            scratch_shapes=[pltpu.VMEM((len(ks) * SIDE * SIDE * n, width), BF)],
        ),
        out_shape=(jax.ShapeDtypeStruct if last else pltpu.VMEM)((2 * half, width), F32),
        compiler_params=params(28),
        cost_estimate=FREE,
        name="weight_grads",
    )(col, *mine, *other, *parts, *([before] if last else []))


def shards(inputs, weight, bias, cotangent):
    tok, feats = inputs.shape
    n = tok // ROWS
    width = weight.shape[1] // (SIDE * SIDE)
    r, c, d = lax.axis_index("row"), lax.axis_index("col"), lax.axis_index("depth")
    z, y = d // SIDE, d % SIDE
    way = 1 - 2 * c
    order = [(r - way * k + 2 * ROWS) % ROWS for k in range(ROWS)]
    inputs = pltpu.with_memory_space_constraint(inputs, pltpu.HBM)
    bias = pltpu.with_memory_space_constraint(bias.reshape(1, -1), pltpu.HBM)
    s0, s1 = [
        jnp.stack(
            [((z + way * kz + SIDE) % SIDE) * 2 + p for kz in chunk for p in range(2)] + order + [c]
        ).astype(jnp.int32)
        for chunk in CHUNKS
    ]
    col = jnp.stack([c]).astype(jnp.int32)
    ys = [(y + way * k + SIDE) % SIDE for k in range(SIDE)]

    def to_column(at, grad, chunk):
        return [
            (grad[j * SIDE : (j + 1) * SIDE] if kz == 0 else at[kz]) for j, kz in enumerate(chunk)
        ]

    def for_y(pieces, k):
        return jnp.stack(
            [lax.dynamic_index_in_dim(p, ys[k], 0, keepdims=False) for p in pieces]
        )

    own0, *send0, token0, x = forward(s0, inputs, weight, width, True)
    got0 = [shift_row(send0[k - 1], -k) for k in (2, 1, 3)]
    x_y1 = shift_y(x, 1)
    own1, *send1, token1 = forward(s1, inputs, weight, width, False, token0)
    got1 = [shift_row(send1[k - 1], -k) for k in (2, 1, 3)]
    x = jnp.concatenate([x, after(x_y1, token1)], axis=0)
    x = jnp.concatenate([x, shift_y(x, 2)], axis=0)

    grad0, act = gelu(s0, got0, own0, bias, cotangent, None, token1)
    line0 = [grad0, shift_row(grad0, 1)]
    at0 = {kz: shift_z(grad0[j * SIDE : (j + 1) * SIDE], kz) for j, kz in enumerate(CHUNKS[0])}
    grad1, act = gelu(s1, got1, own1, bias, cotangent, act)
    x = after(x, grad1)
    mine = {1: shift_z(x, 1)}
    line0.append(shift_row(line0[1], 1))
    line1 = [grad1, shift_row(grad1, 1)]
    at1 = {
        kz: shift_z(grad1[j * SIDE : (j + 1) * SIDE], kz)
        for j, kz in enumerate(CHUNKS[1])
        if kz
    }
    at1 = {kz: after(v, line0[2]) for kz, v in at1.items()}
    pieces = to_column(at0, grad0, CHUNKS[0]) + to_column(at1, grad1, CHUNKS[1])
    held = [for_y(pieces, k) for k in range(SIDE)]
    held = [held[0]] + [shift_y(held[k], k) for k in range(1, SIDE)]
    line0.append(shift_row(line0[2], 1))
    line1.append(shift_row(line1[1], 1))
    line1.append(shift_row(line1[2], 1))

    rows = jnp.stack(held)
    near = [shift_row(rows, 1), shift_row(rows, 3)]
    mine[0] = after(x, *at1.values())
    mine[2] = shift_z(mine[0], 2)
    mine[3] = shift_z(mine[0], 3)
    before, token = input_grads(s0, line0, weight, None, rows)
    own_part, other_part, token = input_grads(s1, line1, weight, before)
    mine = {kz: after(v, token) for kz, v in mine.items()}
    other = {kz: swap(mine[kz]) for kz in range(SIDE)}
    cut = SIDE // 2
    far = [
        shift_row(after(near[0][:cut], token), 1),
        shift_row(after(near[1][cut:], token), 3),
    ]
    input_grad = (own_part + swap(other_part)).astype(BF)

    factor = float(tok * lax.axis_size("depth")) ** (-0.5)
    mine = [mine[kz] for kz in range(SIDE)]
    other = [other[kz] for kz in range(SIDE)]
    most = weight_grads(col, (0, 1, 3), mine, other, (rows, *near), None, 384, factor)
    weight_grad = weight_grads(col, (2,), mine, other, far, most, 384, factor)
    return (act, input_grad, weight_grad)


def solution(mesh):
    return jax.shard_map(
        shards,
        mesh=mesh,
        in_specs=(P("depth", "row"), P("row", "col"), P("col"), P(("depth", "row"), "col")),
        out_specs=(
            P(("depth", "row"), "col"),
            P("depth", ("row", "col")),
            P("row", ("col", "depth")),
        ),
        check_vma=False,
    )
```
